128 devices in a mesh: node: 16 (over x, y), local: 8 (over z, core).
Axes of the slice: x: 4, y: 4, z: 4, core: 2. Of those that a mesh axis runs over, the one named last changes fastest.
Arguments:
- tokens: bfloat16 [16384, 4096], P(('node', 'local')), may hold values from -6 to 6
- expert_ids: int32 [16384, 8], P(('node', 'local')), may hold values from 0 to 127, all different within a row; in each aligned block of 128 rows (0 to 127, 128 to 255, ...) at most 10 rows name the same one
- route_probs: float32 [16384, 8], P(('node', 'local')), may hold values from 0.02 to 0.4
- cotangent: bfloat16 [16384, 4096], P(('node', 'local')), may hold values from -0.29882812 to 0.29882812
- gate_weight: bfloat16 [128, 4096, 768], P(('node', 'local')), may hold values from -0.09375 to 0.09375
- up_weight: bfloat16 [128, 4096, 768], P(('node', 'local')), may hold values from -0.09375 to 0.09375
- down_weight: bfloat16 [128, 768, 4096], P(('node', 'local')), may hold values from -0.21875 to 0.21875
Outputs:
- mixed_out: bfloat16 [16384, 4096], P(('node', 'local'))
- prob_grads: float32 [16384, 8], P(('node', 'local'))
The draws below stay inside these ranges and needn't reach their ends.
Inputs may be any that keep to these rules, and one draw needn't show every extreme that they name: `expert_ids`: each row names 8 different experts. No expert is named by more than 10 of the rows of one device, a bound that some block reaches.
All inputs are finite; a program needn't handle non-finite values.
Results may differ from the reference program's by a relative error of at most 0.0058.
Values may be sent and summed in bfloat16 or wider, within the bound.
No kernel may reach another device: no remote copies, remote signals or barrier semaphores. Data moves between devices by JAX's collectives and lax.ppermute only.
A program may use at most 192 MiB of HBM per device.

```python
import math
import jax
import jax.numpy as jnp
import numpy as np
from jax import lax

D = 4096
TOP = 8
FF = 768
TOK_DEV = 128
EXPERTS = 128
TOKENS = 16384
CAP = 10
N_NODE = 16
N_LOCAL = 8


def block_levels(own_key, extent, pieces, smallest, high):
    def one(position, shards_of):
        heights = jax.random.uniform(jax.random.fold_in(jax.random.fold_in(own_key, 6), position), (shards_of,), jnp.float32, smallest / len(pieces), high / len(pieces))
        return jnp.repeat(jnp.exp(heights), extent[position] // shards_of).reshape((-1,) + (1,) * (len(extent) - position - 1))

    factor_of = one(*pieces[0])
    for cut in pieces[1:]:
        factor_of = factor_of * one(*cut)
    return factor_of


def shared_out(rng, own, number, rows, amount, top, limit, skew):
    order = jax.random.permutation(rng, amount)
    crowded, usual = shares(amount, rows * top, limit, skew, True), shares(amount, rows * top, limit, skew, False)
    places = jnp.arange(amount)

    def named(sizes, offset_by):
        used = int((sizes > 0).sum())
        fixed = max(1, used // 4)
        passed = fixed + (places - fixed + offset_by * (used - fixed)) % max(1, amount - fixed)
        return jnp.zeros((amount,), jnp.int32).at[order[jnp.where(places < fixed, places, passed)]].set(jnp.asarray(sizes, jnp.int32))

    sizes = jnp.where(number % 4 == 0, named(crowded, number // 4), named(usual, number - number // 4 - 1))
    mixed = jax.random.permutation(jax.random.fold_in(own, 3), amount)
    donor, receiver = mixed[0:amount // 2 * 2:2], mixed[1:amount // 2 * 2:2]
    margin = jnp.minimum(sizes[donor] - 1, limit - sizes[receiver]) // 2
    margin = jnp.where((donor == order[0]) | (receiver == order[0]) | (sizes[receiver] == 0), 0, jnp.maximum(margin, 0))
    passed = jax.random.randint(jax.random.fold_in(own, 4), (amount // 2,), 0, 1 << 20) % (margin + 1)
    sizes = sizes.at[donor].add(-passed).at[receiver].add(passed)
    items = jnp.searchsorted(jnp.cumsum(sizes), jnp.arange(rows * top), side="right").astype(jnp.int32)
    table = items.reshape(top, rows).T
    table = table[jax.random.permutation(jax.random.fold_in(own, 1), rows)]
    offset_by = jax.random.randint(jax.random.fold_in(own, 2), (rows, 1), 0, top)
    return jnp.take_along_axis(table, (jnp.arange(top)[None, :] + offset_by) % top, axis=1)


def shares(number_of, total, most, slope, full):
    loads = [(1 << 20) // math.isqrt(standing ** slope) + 1 for standing in range(1, number_of + 1)]
    largest = most if full else min(most, max(-(-total // number_of), total * loads[0] // sum(loads)))
    least = 1 if total - largest >= number_of - 1 else 0
    holding, rest = [largest] + [least] * (number_of - 1), total - largest - least * (number_of - 1)
    while rest > 0:
        candidates = [i for i in range(1, number_of) if holding[i] < largest] or [i for i in range(1, number_of) if holding[i] < most]
        pool, left = sum([loads[i] for i in candidates]), rest
        for i in candidates:
            more = min(most - holding[i], max(1, left * loads[i] // pool), rest)
            holding[i] = holding[i] + more
            rest = rest - more
    return np.array(holding)


def scatter_about(key, dims, spread, reach, cuts=(), kind=jnp.bfloat16):
    values = jax.random.normal(key, dims, jnp.float32) * spread
    if len(cuts) > 0:
        values = block_levels(key, dims, cuts, -0.22, 0.18) * values
    return jnp.clip(values, min=-reach, max=reach).astype(kind)


def setup_inputs(seed: int = 0) -> dict:
    streams_of = jax.random.split(jax.random.key(seed), 8)
    tokens = scatter_about(streams_of[0], (TOKENS, D), 1.0, 6.0, ((0, 128),))
    expert_ids_keys = jax.random.split(jax.random.fold_in(streams_of[1], 1), TOKENS // TOK_DEV)
    expert_ids_turns = jax.random.permutation(jax.random.fold_in(streams_of[1], 3), TOKENS // TOK_DEV)
    expert_ids = jax.vmap(lambda own, number: shared_out(jax.random.fold_in(streams_of[1], 2), own, number, TOK_DEV, EXPERTS, TOP, CAP, 2))(expert_ids_keys, expert_ids_turns).reshape((TOKENS, TOP))
    route_probs = jnp.clip(jnp.exp(math.log(0.4) - 2.9957323 * jax.random.uniform(streams_of[2], (TOKENS, TOP), jnp.float32) ** block_levels(streams_of[2], (TOKENS, TOP), ((0, 128),), -0.2, 0.2)), 0.02, 0.4)
    cotangent = scatter_about(streams_of[3], (TOKENS, D), 0.05, 0.29882812, ((0, 128),))
    gate_weight = scatter_about(streams_of[4], (EXPERTS, D, FF), D ** -0.5, 0.09375, ((0, 128),))
    up_weight = scatter_about(streams_of[5], (EXPERTS, D, FF), D ** -0.5, 0.09375, ((0, 128),))
    down_weight = scatter_about(streams_of[6], (EXPERTS, FF, D), FF ** -0.5, 0.21875, ((0, 128),))
    return dict(tokens=tokens, expert_ids=expert_ids, route_probs=route_probs, cotangent=cotangent, gate_weight=gate_weight, up_weight=up_weight, down_weight=down_weight)


def reference(tokens, expert_ids, route_probs, cotangent, gate_weight, up_weight, down_weight):
    pair_count = TOKENS * TOP
    slot_count = CAP * N_NODE * N_LOCAL
    pair_experts = expert_ids.reshape(-1).astype(jnp.int32)
    one_hot = (pair_experts[:, None] == jnp.arange(EXPERTS, dtype=jnp.int32)[None, :]).astype(jnp.int32)
    rank_in = jnp.sum((jnp.cumsum(one_hot, axis=0) - one_hot) * one_hot, axis=1).astype(jnp.int32)
    slot_pairs = jnp.full((EXPERTS, slot_count), pair_count, jnp.int32)
    slot_pairs = slot_pairs.at[pair_experts, rank_in].set(jnp.arange(pair_count, dtype=jnp.int32))
    probs_flat = route_probs.reshape(-1)

    def expert_step(state, inputs):
        mixed_sum, grad_sum = state
        pair_ids, gate_mat, up_mat, down_mat = inputs
        valid_mask = (pair_ids < pair_count).astype(jnp.float32)
        safe_ids = jnp.minimum(pair_ids, pair_count - 1).astype(jnp.int32)
        token_ids = (safe_ids // TOP).astype(jnp.int32)
        token_rows = tokens[token_ids]
        gate_act = jnp.dot(token_rows, gate_mat, preferred_element_type=jnp.float32)
        up_act = jnp.dot(token_rows, up_mat, preferred_element_type=jnp.float32)
        hidden = (jax.nn.silu(gate_act) * up_act).astype(jnp.bfloat16)
        expert_out = jnp.dot(hidden, down_mat, preferred_element_type=jnp.float32).astype(jnp.bfloat16)
        out_full = expert_out.astype(jnp.float32) * valid_mask[:, None]
        pair_probs = probs_flat[safe_ids].astype(jnp.float32)
        mixed_sum = mixed_sum.at[token_ids].add(pair_probs[:, None] * out_full)
        inner = jnp.sum(cotangent[token_ids].astype(jnp.float32) * out_full, axis=1)
        grad_sum = grad_sum.at[safe_ids].add(inner)
        return (mixed_sum, grad_sum), None

    start_state = (jnp.zeros((TOKENS, D), jnp.float32), jnp.zeros((pair_count,), jnp.float32))
    final_state, unused = lax.scan(expert_step, start_state, (slot_pairs, gate_weight, up_weight, down_weight))
    mixed_sum, grad_sum = final_state
    return mixed_sum.astype(jnp.bfloat16), grad_sum.reshape(TOKENS, TOP)
```

```python
import functools

import jax
import jax.numpy as jnp
from jax import lax
from jax.experimental import pallas as pl
from jax.experimental.pallas import tpu as pltpu
from jax.sharding import PartitionSpec as P

CAP = 10
QUARTERS = 4
MIB = 1 << 20


def iota(shape, dim):
    return lax.broadcasted_iota(jnp.int32, shape, dim)


def dot(a, b, dims=((1,), (0,))):
    return lax.dot_general(a, b, (dims, ((), ())), preferred_element_type=jnp.float32)


def to_quarters(rows):
    slots = rows // QUARTERS
    out, src = iota((rows, rows), 0), iota((rows, rows), 1)
    return (src == (out % slots) * QUARTERS + out // slots).astype(jnp.bfloat16)


def to_slots(rows):
    slots = rows // QUARTERS
    out, src = iota((rows, rows), 0), iota((rows, rows), 1)
    return (src == (out % QUARTERS) * slots + out // QUARTERS).astype(jnp.bfloat16)


def pack_kernel(experts, group, ids_ref, tokens_ref, out_ref, slot_ref, place, quartered):
    step = pl.program_id(0)
    tok = tokens_ref.shape[0]
    width = tokens_ref.shape[1] // QUARTERS

    @pl.when(step == 0)
    def _():
        ids = ids_ref[...]
        named = jnp.zeros((experts, tok), jnp.float32)
        for k in range(ids.shape[0]):
            named += (iota((experts, tok), 0) == ids[k : k + 1, :]).astype(jnp.float32)
        before = (iota((tok, tok), 0) < iota((tok, tok), 1)).astype(jnp.bfloat16)
        rank = dot(named.astype(jnp.bfloat16), before)
        place[...] = jnp.where(named > 0.5, rank, -1.0)
        slot_of = (rank + (iota((experts, tok), 0) * CAP).astype(jnp.float32)).astype(jnp.int32)
        for k in range(ids.shape[0]):
            chosen = iota((experts, tok), 0) == ids[k : k + 1, :]
            slot_ref[k : k + 1, :] = jnp.sum(jnp.where(chosen, slot_of, 0), axis=0, keepdims=True)
        for q in range(QUARTERS):
            quartered[q * tok : (q + 1) * tok, :] = tokens_ref[:, q * width : (q + 1) * width]

    rows = CAP * QUARTERS
    row, col = iota((rows, QUARTERS * tok), 0), iota((rows, QUARTERS * tok), 1)
    wanted = jnp.where(row % QUARTERS == col // tok, row // QUARTERS, -2).astype(jnp.float32)
    mine = place[pl.ds(pl.multiple_of(step * group, group), group), :]
    mine = jnp.concatenate([mine] * QUARTERS, axis=1)
    picks = [
        (mine[g : g + 1, :] == wanted).astype(jnp.float32).astype(jnp.bfloat16) for g in range(group)
    ]
    out_ref[...] = dot(jnp.concatenate(picks, axis=0), quartered[...]).astype(jnp.bfloat16)


def pack(ids_t, tokens, experts):
    tok, model = tokens.shape
    group = 16
    rows = CAP * QUARTERS
    width = model // QUARTERS
    return pl.pallas_call(
        functools.partial(pack_kernel, experts, group),
        grid=(experts // group,),
        in_specs=[
            pl.BlockSpec(ids_t.shape, lambda i: (0, 0)),
            pl.BlockSpec(tokens.shape, lambda i: (0, 0)),
        ],
        out_specs=[
            pl.BlockSpec((group * rows, width), lambda i: (i, 0)),
            pl.BlockSpec(ids_t.shape, lambda i: (0, 0)),
        ],
        out_shape=[
            jax.ShapeDtypeStruct((experts * rows, width), jnp.bfloat16),
            jax.ShapeDtypeStruct(ids_t.shape, jnp.int32),
        ],
        scratch_shapes=[
            pltpu.VMEM((experts, tok), jnp.float32),
            pltpu.VMEM((QUARTERS * tok, width), jnp.bfloat16),
        ],
        compiler_params=pltpu.CompilerParams(vmem_limit_bytes=40 * MIB),
    )(ids_t, tokens)


SUB = 256


def expert_kernel(x_ref, gate_hbm, up_hbm, down_hbm, y_ref, gate, up, down, xs, sems):
    step = pl.program_id(0)
    block = xs.shape[0]
    model, ff = gate.shape
    width = model // QUARTERS
    per = SUB // QUARTERS

    quarters = [pl.ds(q * width, width) for q in range(QUARTERS)]
    gates = [pltpu.make_async_copy(gate_hbm.at[p, :], gate.at[p, :], sems.at[0, q]) for q, p in enumerate(quarters)]
    ups = [pltpu.make_async_copy(up_hbm.at[p, :], up.at[p, :], sems.at[1, q]) for q, p in enumerate(quarters)]
    downs = pltpu.make_async_copy(down_hbm, down, sems.at[2, 0])

    def wait(*copies):
        @pl.when(step == 0)
        def _():
            for copy in copies:
                copy.wait()

    @pl.when(step == 0)
    def _():
        for q in range(QUARTERS):
            gates[q].start()
            ups[q].start()
        downs.start()

    order = to_quarters(SUB)
    for b in range(block // per):
        part = dot(order, x_ref[b * SUB : (b + 1) * SUB, :]).astype(jnp.bfloat16)
        for q in range(QUARTERS):
            xs[b * per : (b + 1) * per, q * width : (q + 1) * width] = part[q * per : (q + 1) * per, :]

    gate_act = jnp.zeros((block, ff), jnp.float32)
    up_act = jnp.zeros((block, ff), jnp.float32)
    for q in range(QUARTERS):
        part = slice(q * width, (q + 1) * width)
        wait(gates[q], ups[q])
        gate_act += dot(xs[:, part], gate[part, :])
        up_act += dot(xs[:, part], up[part, :])
    hidden = (gate_act / (1.0 + jnp.exp(-gate_act)) * up_act).astype(jnp.bfloat16)
    wait(downs)
    for q in range(QUARTERS):
        part = slice(q * width, (q + 1) * width)
        xs[:, part] = dot(hidden, down[:, part]).astype(jnp.bfloat16)
    back = to_slots(SUB)
    for b in range(block // per):
        part = jnp.concatenate(
            [xs[b * per : (b + 1) * per, q * width : (q + 1) * width] for q in range(QUARTERS)], axis=0
        )
        y_ref[b * SUB : (b + 1) * SUB, :] = dot(back, part).astype(jnp.bfloat16)


def expert_apply(x, gate, up, down, block=256):
    model, ff = gate.shape
    width = model // QUARTERS
    rows = x.shape[0]
    return pl.pallas_call(
        expert_kernel,
        grid=(rows // (block * QUARTERS),),
        in_specs=[pl.BlockSpec((block * QUARTERS, width), lambda i: (i, 0))]
        + [pl.BlockSpec(memory_space=pl.ANY)] * 3,
        out_specs=pl.BlockSpec((block * QUARTERS, width), lambda i: (i, 0)),
        out_shape=jax.ShapeDtypeStruct(x.shape, jnp.bfloat16),
        scratch_shapes=[
            pltpu.VMEM(gate.shape, jnp.bfloat16),
            pltpu.VMEM(up.shape, jnp.bfloat16),
            pltpu.VMEM(down.shape, jnp.bfloat16),
            pltpu.VMEM((block, model), jnp.bfloat16),
            pltpu.SemaphoreType.DMA((3, QUARTERS)),
        ],
        compiler_params=pltpu.CompilerParams(vmem_limit_bytes=60 * MIB),
    )(x, gate, up, down)


def combine_kernel(slot_ref, probs_ref, cot_ref, y_ref, mixed_ref, grads_ref, xs):
    slots = xs.shape[0]
    tok, model = cot_ref.shape
    width = model // QUARTERS
    per = SUB // QUARTERS
    order = to_quarters(SUB)
    for b in range(slots // per):
        part = dot(order, y_ref[b * SUB : (b + 1) * SUB, :]).astype(jnp.bfloat16)
        for q in range(QUARTERS):
            xs[b * per : (b + 1) * per, q * width : (q + 1) * width] = part[q * per : (q + 1) * per, :]
    inner = dot(xs[...], cot_ref[...], ((1,), (1,)))
    here = iota((slots, tok), 0)
    weight = jnp.zeros((slots, tok), jnp.float32)
    for k in range(slot_ref.shape[0]):
        mask = here == slot_ref[k : k + 1, :]
        weight += jnp.where(mask, probs_ref[k : k + 1, :], 0.0)
        grads_ref[k : k + 1, :] = jnp.sum(jnp.where(mask, inner, 0.0), axis=0, keepdims=True)
    weight = weight.T
    high = weight.astype(jnp.bfloat16)
    low = (weight - high.astype(jnp.float32)).astype(jnp.bfloat16)
    both = jnp.concatenate([high, low], axis=0)
    for q in range(QUARTERS):
        part = slice(q * width, (q + 1) * width)
        total = dot(both, xs[:, part])
        mixed_ref[:, part] = (total[:tok] + total[tok:]).astype(jnp.bfloat16)


def combine(slot_t, probs_t, cotangent, y):
    model = cotangent.shape[1]
    return pl.pallas_call(
        combine_kernel,
        out_shape=[
            jax.ShapeDtypeStruct(cotangent.shape, jnp.bfloat16),
            jax.ShapeDtypeStruct(probs_t.shape, jnp.float32),
        ],
        scratch_shapes=[pltpu.VMEM((y.shape[0] // QUARTERS, model), jnp.bfloat16)],
        compiler_params=pltpu.CompilerParams(vmem_limit_bytes=40 * MIB),
    )(slot_t, probs_t, cotangent, y)


def exchange(rows, devices):
    parts = rows.reshape(devices, rows.shape[0] // devices, rows.shape[1])
    parts = lax.all_to_all(parts, ("node", "local"), split_axis=0, concat_axis=0, tiled=True)
    return parts.reshape(rows.shape)


def per_device(tokens, expert_ids, route_probs, cotangent, gate_weight, up_weight, down_weight):
    devices = lax.axis_size("node") * lax.axis_size("local")
    packed, slot_t = pack(expert_ids.T, tokens, devices)
    received = exchange(packed, devices)
    results = expert_apply(received, gate_weight[0], up_weight[0], down_weight[0])
    returned = exchange(results, devices)
    mixed, grads_t = combine(slot_t, route_probs.T, cotangent, returned)
    return mixed, grads_t.T


def solution(mesh):
    placed = (P(("node", "local"), None),) * 4 + (P(("node", "local"), None, None),) * 3
    return jax.shard_map(
        per_device,
        mesh=mesh,
        in_specs=placed,
        out_specs=(P(("node", "local"), None), P(("node", "local"), None)),
        check_vma=False,
    )
```

```python
import functools

import jax
import jax.numpy as jnp
from jax import lax
from jax.experimental import pallas as pl
from jax.experimental.pallas import tpu as pltpu
from jax.sharding import PartitionSpec as P

CAP = 10
QUARTERS = 4
MAIN = 8
TAIL = CAP - MAIN
ROWS = CAP * QUARTERS
MIB = 1 << 20


def iota(shape, dim):
    return lax.broadcasted_iota(jnp.int32, shape, dim)


def dot(a, b, dims=((1,), (0,))):
    return lax.dot_general(a, b, (dims, ((), ())), preferred_element_type=jnp.float32)


def to_quarters(rows):
    slots = rows // QUARTERS
    out, src = iota((rows, rows), 0), iota((rows, rows), 1)
    return (src == (out % slots) * QUARTERS + out // slots).astype(jnp.bfloat16)


def to_slots(rows):
    slots = rows // QUARTERS
    out, src = iota((rows, rows), 0), iota((rows, rows), 1)
    return (src == (out % QUARTERS) * slots + out // QUARTERS).astype(jnp.bfloat16)


def unpack(messages, x_ref, xs, tails):
    width = x_ref.shape[1]
    for pair in range(messages // 2):
        both = x_ref[pair * 2 * ROWS : (pair + 1) * 2 * ROWS, :].astype(jnp.float32)
        for q in range(QUARTERS + 1):
            first = both[q * MAIN : (q + 1) * MAIN, :]
            second = both[ROWS + q * MAIN : ROWS + (q + 1) * MAIN, :]
            rows = jnp.concatenate([first, second], axis=0).astype(jnp.bfloat16)
            if q < QUARTERS:
                xs[pair * 2 * MAIN : (pair + 1) * 2 * MAIN, q * width : (q + 1) * width] = rows
            else:
                tails[pair * 2 * MAIN : (pair + 1) * 2 * MAIN, :] = rows
    sub = 32 * MAIN
    per = sub // QUARTERS
    order = to_quarters(sub)
    for b in range(messages // 32):
        part = dot(order, tails[b * sub : (b + 1) * sub, :]).astype(jnp.bfloat16)
        base = messages * MAIN + b * per
        for q in range(QUARTERS):
            xs[base : base + per, q * width : (q + 1) * width] = part[q * per : (q + 1) * per, :]


def pack_kernel(experts, group, ids_ref, tokens_ref, out_ref, slot_ref, place, quartered):
    step = pl.program_id(0)
    tok = tokens_ref.shape[0]
    width = tokens_ref.shape[1] // QUARTERS

    @pl.when(step == 0)
    def _():
        ids = ids_ref[...]
        expert = iota((experts, tok), 0)
        named = jnp.zeros((experts, tok), jnp.float32)
        for k in range(ids.shape[0]):
            named += (expert == ids[k : k + 1, :]).astype(jnp.float32)
        before = (iota((tok, tok), 0) < iota((tok, tok), 1)).astype(jnp.bfloat16)
        rank = dot(named.astype(jnp.bfloat16), before)
        place[...] = jnp.where(named > 0.5, rank, -1.0)
        rank = rank.astype(jnp.int32)
        slot_of = jnp.where(rank < MAIN, expert * MAIN + rank, experts * MAIN + expert * TAIL + rank - MAIN)
        for k in range(ids.shape[0]):
            chosen = expert == ids[k : k + 1, :]
            slot_ref[k : k + 1, :] = jnp.sum(jnp.where(chosen, slot_of, 0), axis=0, keepdims=True)
        for q in range(QUARTERS):
            quartered[q * tok : (q + 1) * tok, :] = tokens_ref[:, q * width : (q + 1) * width]

    mine = place[pl.ds(pl.multiple_of(step * group, group), group), :]
    wide = jnp.concatenate([mine] * QUARTERS, axis=1)
    rank = iota((MAIN, tok), 0).astype(jnp.float32)
    row, col = iota((MAIN, QUARTERS * tok), 0), iota((MAIN, QUARTERS * tok), 1)
    late = jnp.where(row % QUARTERS == col // tok, MAIN + row // QUARTERS, -2).astype(jnp.float32)
    main = [(mine[g : g + 1, :] == rank).astype(jnp.float32) for g in range(group)]
    tail = [(wide[g : g + 1, :] == late).astype(jnp.float32) for g in range(group)]
    main = jnp.concatenate(main, axis=0).astype(jnp.bfloat16)
    tail = jnp.concatenate(tail, axis=0).astype(jnp.bfloat16)
    parts = [dot(main, quartered[q * tok : (q + 1) * tok, :]) for q in range(QUARTERS)]
    parts.append(dot(tail, quartered[...]))
    for pair in range(group // 2):
        both = [p[(2 * pair + g) * MAIN : (2 * pair + g + 1) * MAIN, :] for g in range(2) for p in parts]
        out_ref[pair * 2 * ROWS : (pair + 1) * 2 * ROWS, :] = jnp.concatenate(both, axis=0).astype(jnp.bfloat16)


def pack(ids_t, tokens, experts):
    tok, model = tokens.shape
    group = 32
    width = model // QUARTERS
    return pl.pallas_call(
        functools.partial(pack_kernel, experts, group),
        grid=(experts // group,),
        in_specs=[
            pl.BlockSpec(ids_t.shape, lambda i: (0, 0)),
            pl.BlockSpec(tokens.shape, lambda i: (0, 0)),
        ],
        out_specs=[
            pl.BlockSpec((group * ROWS, width), lambda i: (i, 0)),
            pl.BlockSpec(ids_t.shape, lambda i: (0, 0)),
        ],
        out_shape=[
            jax.ShapeDtypeStruct((experts * ROWS, width), jnp.bfloat16),
            jax.ShapeDtypeStruct(ids_t.shape, jnp.int32),
        ],
        scratch_shapes=[
            pltpu.VMEM((experts, tok), jnp.float32),
            pltpu.VMEM((QUARTERS * tok, width), jnp.bfloat16),
        ],
        compiler_params=pltpu.CompilerParams(vmem_limit_bytes=40 * MIB),
    )(ids_t, tokens)


def expert_kernel(x_ref, gate_hbm, up_hbm, down_hbm, y_ref, gate, up, down, xs, ys, tails, sems):
    step = pl.program_id(0)
    block = xs.shape[0]
    messages = block // CAP
    model, ff = gate.shape
    width = model // QUARTERS

    quarters = [pl.ds(q * width, width) for q in range(QUARTERS)]
    gates = [pltpu.make_async_copy(gate_hbm.at[p, :], gate.at[p, :], sems.at[0, q]) for q, p in enumerate(quarters)]
    ups = [pltpu.make_async_copy(up_hbm.at[p, :], up.at[p, :], sems.at[1, q]) for q, p in enumerate(quarters)]
    downs = pltpu.make_async_copy(down_hbm, down, sems.at[2, 0])

    def wait(*copies):
        @pl.when(step == 0)
        def _():
            for copy in copies:
                copy.wait()

    @pl.when(step == 0)
    def _():
        for q in range(QUARTERS):
            gates[q].start()
            ups[q].start()
        downs.start()

    unpack(messages, x_ref, xs, tails)
    gate_act = jnp.zeros((block, ff), jnp.float32)
    up_act = jnp.zeros((block, ff), jnp.float32)
    for q in range(QUARTERS):
        part = slice(q * width, (q + 1) * width)
        wait(gates[q], ups[q])
        gate_act += dot(xs[:, part], gate[part, :])
        up_act += dot(xs[:, part], up[part, :])
    hidden = (gate_act / (1.0 + jnp.exp(-gate_act)) * up_act).astype(jnp.bfloat16)
    wait(downs)
    for q in range(QUARTERS):
        part = slice(q * width, (q + 1) * width)
        ys[:, part] = dot(hidden, down[:, part])
    main = messages * MAIN
    late = [ys[main:, q * width : (q + 1) * width].astype(jnp.bfloat16) for q in range(QUARTERS)]
    late = dot(to_slots(messages * MAIN), jnp.concatenate(late, axis=0))
    for pair in range(messages // 2):
        both = []
        for m in (2 * pair, 2 * pair + 1):
            both += [ys[m * MAIN : (m + 1) * MAIN, q * width : (q + 1) * width] for q in range(QUARTERS)]
            both.append(late[m * MAIN : (m + 1) * MAIN, :])
        y_ref[pair * 2 * ROWS : (pair + 1) * 2 * ROWS, :] = jnp.concatenate(both, axis=0).astype(jnp.bfloat16)


def expert_apply(x, gate, up, down, messages=32):
    model, ff = gate.shape
    width = model // QUARTERS
    block = messages * CAP
    return pl.pallas_call(
        expert_kernel,
        grid=(x.shape[0] // (messages * ROWS),),
        in_specs=[pl.BlockSpec((messages * ROWS, width), lambda i: (i, 0))]
        + [pl.BlockSpec(memory_space=pl.ANY)] * 3,
        out_specs=pl.BlockSpec((messages * ROWS, width), lambda i: (i, 0)),
        out_shape=jax.ShapeDtypeStruct(x.shape, jnp.bfloat16),
        scratch_shapes=[
            pltpu.VMEM(gate.shape, jnp.bfloat16),
            pltpu.VMEM(up.shape, jnp.bfloat16),
            pltpu.VMEM(down.shape, jnp.bfloat16),
            pltpu.VMEM((block, model), jnp.bfloat16),
            pltpu.VMEM((block, model), jnp.float32),
            pltpu.VMEM((messages * MAIN, width), jnp.bfloat16),
            pltpu.SemaphoreType.DMA((3, QUARTERS)),
        ],
        compiler_params=pltpu.CompilerParams(vmem_limit_bytes=60 * MIB),
    )(x, gate, up, down)


def combine_kernel(slot_ref, probs_ref, cot_ref, y_ref, mixed_ref, grads_ref, xs, tails):
    slots = xs.shape[0]
    tok, model = cot_ref.shape
    width = model // QUARTERS
    unpack(slots // CAP, y_ref, xs, tails)
    inner = dot(xs[...], cot_ref[...], ((1,), (1,)))
    here = iota((slots, tok), 0)
    weight = jnp.zeros((slots, tok), jnp.float32)
    for k in range(slot_ref.shape[0]):
        mask = here == slot_ref[k : k + 1, :]
        weight += jnp.where(mask, probs_ref[k : k + 1, :], 0.0)
        grads_ref[k : k + 1, :] = jnp.sum(jnp.where(mask, inner, 0.0), axis=0, keepdims=True)
    weight = weight.T
    high = weight.astype(jnp.bfloat16)
    low = (weight - high.astype(jnp.float32)).astype(jnp.bfloat16)
    both = jnp.concatenate([high, low], axis=0)
    for q in range(QUARTERS):
        part = slice(q * width, (q + 1) * width)
        total = dot(both, xs[:, part])
        mixed_ref[:, part] = (total[:tok] + total[tok:]).astype(jnp.bfloat16)


def combine(slot_t, probs_t, cotangent, y):
    model = cotangent.shape[1]
    slots = y.shape[0] // QUARTERS
    return pl.pallas_call(
        combine_kernel,
        out_shape=[
            jax.ShapeDtypeStruct(cotangent.shape, jnp.bfloat16),
            jax.ShapeDtypeStruct(probs_t.shape, jnp.float32),
        ],
        scratch_shapes=[
            pltpu.VMEM((slots, model), jnp.bfloat16),
            pltpu.VMEM((slots // CAP * MAIN, y.shape[1]), jnp.bfloat16),
        ],
        compiler_params=pltpu.CompilerParams(vmem_limit_bytes=40 * MIB),
    )(slot_t, probs_t, cotangent, y)


def exchange(rows, devices):
    parts = rows.reshape(devices, rows.shape[0] // devices, rows.shape[1])
    parts = lax.all_to_all(parts, ("node", "local"), split_axis=0, concat_axis=0, tiled=True)
    return parts.reshape(rows.shape)


def per_device(tokens, expert_ids, route_probs, cotangent, gate_weight, up_weight, down_weight):
    devices = lax.axis_size("node") * lax.axis_size("local")
    packed, slot_t = pack(expert_ids.T, tokens, devices)
    received = exchange(packed, devices)
    results = expert_apply(received, gate_weight[0], up_weight[0], down_weight[0])
    returned = exchange(results, devices)
    mixed, grads_t = combine(slot_t, route_probs.T, cotangent, returned)
    return mixed, grads_t.T


def solution(mesh):
    placed = (P(("node", "local"), None),) * 4 + (P(("node", "local"), None, None),) * 3
    return jax.shard_map(
        per_device,
        mesh=mesh,
        in_specs=placed,
        out_specs=(P(("node", "local"), None), P(("node", "local"), None)),
        check_vma=False,
    )
```

```python
import functools

import jax
import jax.numpy as jnp
from jax import lax
from jax.experimental import pallas as pl
from jax.experimental.pallas import tpu as pltpu
from jax.sharding import PartitionSpec as P

CAP = 10
PARTS = 8
MAIN = 8
TAIL = CAP - MAIN
TILE = 2 * MAIN
BODY = PARTS * MAIN
ROWS = CAP * PARTS
SUB = 256
MIB = 1 << 20


def iota(shape, dim):
    return lax.broadcasted_iota(jnp.int32, shape, dim)


def dot(a, b, dims=((1,), (0,))):
    return lax.dot_general(a, b, (dims, ((), ())), preferred_element_type=jnp.float32)


def tails_in(x_ref, xs, base):
    width = x_ref.shape[2]
    slots = SUB // PARTS
    out, src = iota((SUB, SUB), 0), iota((SUB, SUB), 1)
    order = (src == (out % slots) * PARTS + out // slots).astype(jnp.bfloat16)
    per = SUB // TILE
    for b in range(x_ref.shape[0] // per):
        rows = x_ref[b * per : (b + 1) * per, BODY:ROWS, :].reshape(SUB, width)
        rows = dot(order, rows).astype(jnp.bfloat16)
        for q in range(PARTS):
            xs[base + b * slots : base + (b + 1) * slots, q * width : (q + 1) * width] = rows[q * slots : (q + 1) * slots, :]


def tails_out(tails, out_ref):
    width = out_ref.shape[2]
    slots = SUB // PARTS
    out, src = iota((SUB, SUB), 0), iota((SUB, SUB), 1)
    order = (src == (out % PARTS) * slots + out // PARTS).astype(jnp.bfloat16)
    per = SUB // TILE
    for b in range(out_ref.shape[0] // per):
        rows = [tails[b * slots : (b + 1) * slots, q * width : (q + 1) * width] for q in range(PARTS)]
        rows = dot(order, jnp.concatenate(rows, axis=0)).astype(jnp.bfloat16)
        out_ref[b * per : (b + 1) * per, BODY:ROWS, :] = rows.reshape(per, TILE, width)


def main_in(x_ref, xs, j, step=32):
    width = x_ref.shape[2]
    for b in range(0, x_ref.shape[0], step):
        both = x_ref[b : b + step, j * TILE : (j + 1) * TILE, :].astype(jnp.float32)
        for half in range(2):
            rows = both[:, half * MAIN : (half + 1) * MAIN, :].reshape(step * MAIN, width)
            q = 2 * j + half
            xs[b * MAIN : (b + step) * MAIN, q * width : (q + 1) * width] = rows.astype(jnp.bfloat16)


def main_out(rows, out_ref, j):
    messages, _, width = out_ref.shape
    halves = [rows[:, h * width : (h + 1) * width].reshape(messages, MAIN, width) for h in range(2)]
    out_ref[:, j * TILE : (j + 1) * TILE, :] = jnp.concatenate(halves, axis=1).astype(jnp.bfloat16)


def pack_kernel(experts, ids_ref, tokens_ref, out_ref, slot_ref, place, tails):
    step = pl.program_id(0)
    tok, model = tokens_ref.shape
    group = out_ref.shape[0]
    span = model // PARTS * 2

    @pl.when(step == 0)
    def _():
        ids = ids_ref[...]
        expert = iota((experts, tok), 0)
        named = jnp.zeros((experts, tok), jnp.float32)
        for k in range(ids.shape[0]):
            named += (expert == ids[k : k + 1, :]).astype(jnp.float32)
        before = (iota((tok, tok), 0) < iota((tok, tok), 1)).astype(jnp.bfloat16)
        rank = dot(named.astype(jnp.bfloat16), before)
        place[...] = jnp.where(named > 0.5, rank, -1.0)
        rank = rank.astype(jnp.int32)
        slot_of = jnp.where(rank < MAIN, expert * MAIN + rank, experts * MAIN + expert * TAIL + rank - MAIN)
        for k in range(ids.shape[0]):
            chosen = expert == ids[k : k + 1, :]
            slot_ref[k : k + 1, :] = jnp.sum(jnp.where(chosen, slot_of, 0), axis=0, keepdims=True)

    mine = place[pl.ds(pl.multiple_of(step * group, group), group), :]
    rank = iota((MAIN, tok), 0).astype(jnp.float32)
    main = [(mine[g : g + 1, :] == rank).astype(jnp.float32) for g in range(group)]
    main = jnp.concatenate(main, axis=0).astype(jnp.bfloat16)
    row = iota((MAIN, tok), 0)
    late = []
    for g in range(0, group, MAIN // TAIL):
        match = jnp.zeros((MAIN, tok), jnp.float32)
        for h in range(MAIN // TAIL):
            rank = jnp.where(row // TAIL == h, MAIN + row % TAIL, -2).astype(jnp.float32)
            match += (mine[g + h : g + h + 1, :] == rank).astype(jnp.float32)
        late.append(match)
    late = jnp.concatenate(late, axis=0).astype(jnp.bfloat16)
    for j in range(PARTS // 2):
        part = slice(j * span, (j + 1) * span)
        tails[:, part] = dot(late, tokens_ref[:, part]).astype(jnp.bfloat16)
        main_out(dot(main, tokens_ref[:, part]), out_ref, j)
    tails_out(tails, out_ref)


def pack(ids_t, tokens, experts):
    tok, model = tokens.shape
    group = 32
    shape = (ROWS, model // PARTS)
    return pl.pallas_call(
        functools.partial(pack_kernel, experts),
        grid=(experts // group,),
        in_specs=[
            pl.BlockSpec(ids_t.shape, lambda i: (0, 0)),
            pl.BlockSpec(tokens.shape, lambda i: (0, 0)),
        ],
        out_specs=[
            pl.BlockSpec((group, *shape), lambda i: (i, 0, 0)),
            pl.BlockSpec(ids_t.shape, lambda i: (0, 0)),
        ],
        out_shape=[
            jax.ShapeDtypeStruct((experts, *shape), jnp.bfloat16),
            jax.ShapeDtypeStruct(ids_t.shape, jnp.int32),
        ],
        scratch_shapes=[
            pltpu.VMEM((experts, tok), jnp.float32),
            pltpu.VMEM((group * TAIL, model), jnp.bfloat16),
        ],
        compiler_params=pltpu.CompilerParams(vmem_limit_bytes=14 * MIB),
    )(ids_t, tokens)


def expert_kernel(x_ref, gate, up, down, y_ref, xs, tails):
    main = x_ref.shape[0] * MAIN
    model = gate.shape[0]
    span = model // PARTS * 2
    tails_in(x_ref, xs, main)
    gate_act, up_act = 0.0, 0.0
    for j in range(PARTS // 2):
        part = slice(j * span, (j + 1) * span)
        main_in(x_ref, xs, j)
        gate_act += dot(xs[:, part], gate[part, :])
        up_act += dot(xs[:, part], up[part, :])
    hidden = (gate_act / (1.0 + jnp.exp(-gate_act)) * up_act).astype(jnp.bfloat16)
    for j in range(PARTS // 2):
        part = slice(j * span, (j + 1) * span)
        result = dot(hidden, down[:, part])
        main_out(result[:main], y_ref, j)
        tails[:, part] = result[main:].astype(jnp.bfloat16)
    tails_out(tails, y_ref)


def expert_apply(x, gate, up, down, messages=32):
    model = gate.shape[0]
    block = pl.BlockSpec((messages, *x.shape[1:]), lambda i: (i, 0, 0))
    return pl.pallas_call(
        expert_kernel,
        grid=(x.shape[0] // messages,),
        in_specs=[block] + [pl.BlockSpec(memory_space=pltpu.VMEM)] * 3,
        out_specs=block,
        out_shape=jax.ShapeDtypeStruct(x.shape, jnp.bfloat16),
        scratch_shapes=[
            pltpu.VMEM((messages * CAP, model), jnp.bfloat16),
            pltpu.VMEM((messages * TAIL, model), jnp.bfloat16),
        ],
        compiler_params=pltpu.CompilerParams(vmem_limit_bytes=24 * MIB),
    )(x, gate, up, down)


def combine_kernel(slot_ref, probs_ref, cot_ref, y_ref, mixed_ref, grads_ref, xs):
    slots, model = xs.shape
    tok = cot_ref.shape[0]
    span = model // PARTS * 2
    here = iota((slots, tok), 0)
    weight = jnp.zeros((slots, tok), jnp.float32)
    for k in range(slot_ref.shape[0]):
        weight += jnp.where(here == slot_ref[k : k + 1, :], probs_ref[k : k + 1, :], 0.0)
    weight = weight.T.astype(jnp.bfloat16)
    tails_in(y_ref, xs, y_ref.shape[0] * MAIN)
    inner = 0.0
    for j in range(PARTS // 2):
        part = slice(j * span, (j + 1) * span)
        main_in(y_ref, xs, j)
        inner += dot(xs[:, part], cot_ref[:, part], ((1,), (1,)))
        mixed_ref[:, part] = dot(weight, xs[:, part]).astype(jnp.bfloat16)
    for k in range(slot_ref.shape[0]):
        mask = here == slot_ref[k : k + 1, :]
        grads_ref[k : k + 1, :] = jnp.sum(jnp.where(mask, inner, 0.0), axis=0, keepdims=True)


def combine(slot_t, probs_t, cotangent, y):
    model = cotangent.shape[1]
    return pl.pallas_call(
        combine_kernel,
        out_shape=[
            jax.ShapeDtypeStruct(cotangent.shape, jnp.bfloat16),
            jax.ShapeDtypeStruct(probs_t.shape, jnp.float32),
        ],
        scratch_shapes=[pltpu.VMEM((y.shape[0] * CAP, model), jnp.bfloat16)],
        compiler_params=pltpu.CompilerParams(vmem_limit_bytes=40 * MIB),
    )(slot_t, probs_t, cotangent, y)


def exchange(messages):
    return lax.all_to_all(messages, ("node", "local"), split_axis=0, concat_axis=0, tiled=True)


def per_device(tokens, expert_ids, route_probs, cotangent, gate_weight, up_weight, down_weight):
    devices = lax.axis_size("node") * lax.axis_size("local")
    packed, slot_t = pack(expert_ids.T, tokens, devices)
    received = exchange(packed)
    results = expert_apply(received, gate_weight[0], up_weight[0], down_weight[0])
    returned = exchange(results)
    mixed, grads_t = combine(slot_t, route_probs.T, cotangent, returned)
    return mixed, grads_t.T


def solution(mesh):
    placed = (P(("node", "local"), None),) * 4 + (P(("node", "local"), None, None),) * 3
    return jax.shard_map(
        per_device,
        mesh=mesh,
        in_specs=placed,
        out_specs=(P(("node", "local"), None), P(("node", "local"), None)),
        check_vma=False,
    )
```

```python
import functools

import jax
import jax.numpy as jnp
from jax import lax
from jax.experimental import pallas as pl
from jax.experimental.pallas import tpu as pltpu
from jax.sharding import PartitionSpec as P

CAP = 10
PARTS = 8
MAIN = 8
TAIL = CAP - MAIN
TILE = 2 * MAIN
BODY = PARTS * MAIN
ROWS = CAP * PARTS
SUB = 256
MIB = 1 << 20


def iota(shape, dim):
    return lax.broadcasted_iota(jnp.int32, shape, dim)


def dot(a, b, dims=((1,), (0,))):
    return lax.dot_general(a, b, (dims, ((), ())), preferred_element_type=jnp.float32)


def tails_in(x_ref, first, xs, base):
    width = x_ref.shape[2]
    slots = SUB // PARTS
    out, src = iota((SUB, SUB), 0), iota((SUB, SUB), 1)
    order = (src == (out % slots) * PARTS + out // slots).astype(jnp.bfloat16)
    per = SUB // TILE
    for b in range(x_ref.shape[0] // per):
        rows = x_ref[b * per : (b + 1) * per, first : first + TILE, :].reshape(SUB, width)
        rows = dot(order, rows).astype(jnp.bfloat16)
        for q in range(PARTS):
            xs[base + b * slots : base + (b + 1) * slots, q * width : (q + 1) * width] = rows[q * slots : (q + 1) * slots, :]


def tails_out(tails, out_ref):
    width = out_ref.shape[2]
    slots = SUB // PARTS
    out, src = iota((SUB, SUB), 0), iota((SUB, SUB), 1)
    order = (src == (out % PARTS) * slots + out // PARTS).astype(jnp.bfloat16)
    per = SUB // TILE
    for b in range(out_ref.shape[0] // per):
        rows = [tails[b * slots : (b + 1) * slots, q * width : (q + 1) * width] for q in range(PARTS)]
        rows = dot(order, jnp.concatenate(rows, axis=0)).astype(jnp.bfloat16)
        out_ref[b * per : (b + 1) * per, :, :] = rows.reshape(per, TILE, width)


def main_in(x_ref, xs, j, step=32):
    width = x_ref.shape[2]
    for b in range(0, x_ref.shape[0], step):
        both = x_ref[b : b + step, j * TILE : (j + 1) * TILE, :].astype(jnp.float32)
        for half in range(2):
            rows = both[:, half * MAIN : (half + 1) * MAIN, :].reshape(step * MAIN, width)
            q = 2 * j + half
            xs[b * MAIN : (b + step) * MAIN, q * width : (q + 1) * width] = rows.astype(jnp.bfloat16)


def main_out(rows, out_ref, j):
    messages, _, width = out_ref.shape
    halves = [rows[:, h * width : (h + 1) * width].reshape(messages, MAIN, width) for h in range(2)]
    out_ref[:, j * TILE : (j + 1) * TILE, :] = jnp.concatenate(halves, axis=1).astype(jnp.bfloat16)


def pack_kernel(experts, ids_ref, tokens_ref, body_ref, tail_ref, slot_ref, place, tails):
    step = pl.program_id(0)
    tok, model = tokens_ref.shape
    group = body_ref.shape[0]
    span = model // PARTS * 2

    @pl.when(step == 0)
    def _():
        ids = ids_ref[...]
        expert = iota((experts, tok), 0)
        named = jnp.zeros((experts, tok), jnp.float32)
        for k in range(ids.shape[0]):
            named += (expert == ids[k : k + 1, :]).astype(jnp.float32)
        before = (iota((tok, tok), 0) < iota((tok, tok), 1)).astype(jnp.bfloat16)
        rank = dot(named.astype(jnp.bfloat16), before)
        place[...] = jnp.where(named > 0.5, rank, -1.0)
        rank = rank.astype(jnp.int32)
        slot_of = jnp.where(rank < MAIN, expert * MAIN + rank, experts * MAIN + expert * TAIL + rank - MAIN)
        for k in range(ids.shape[0]):
            chosen = expert == ids[k : k + 1, :]
            slot_ref[k : k + 1, :] = jnp.sum(jnp.where(chosen, slot_of, 0), axis=0, keepdims=True)

    mine = place[pl.ds(pl.multiple_of(step * group, group), group), :]
    rank = iota((MAIN, tok), 0).astype(jnp.float32)
    main = [(mine[g : g + 1, :] == rank).astype(jnp.float32) for g in range(group)]
    main = jnp.concatenate(main, axis=0).astype(jnp.bfloat16)
    row = iota((MAIN, tok), 0)
    late = []
    for g in range(0, group, MAIN // TAIL):
        match = jnp.zeros((MAIN, tok), jnp.float32)
        for h in range(MAIN // TAIL):
            rank = jnp.where(row // TAIL == h, MAIN + row % TAIL, -2).astype(jnp.float32)
            match += (mine[g + h : g + h + 1, :] == rank).astype(jnp.float32)
        late.append(match)
    late = jnp.concatenate(late, axis=0).astype(jnp.bfloat16)
    for j in range(PARTS // 2):
        part = slice(j * span, (j + 1) * span)
        tails[:, part] = dot(late, tokens_ref[:, part]).astype(jnp.bfloat16)
        main_out(dot(main, tokens_ref[:, part]), body_ref, j)
    tails_out(tails, tail_ref)


def pack(ids_t, tokens, experts):
    tok, model = tokens.shape
    group = 32
    width = model // PARTS
    return pl.pallas_call(
        functools.partial(pack_kernel, experts),
        grid=(experts // group,),
        in_specs=[
            pl.BlockSpec(ids_t.shape, lambda i: (0, 0)),
            pl.BlockSpec(tokens.shape, lambda i: (0, 0)),
        ],
        out_specs=[
            pl.BlockSpec((group, BODY, width), lambda i: (i, 0, 0)),
            pl.BlockSpec((group, TILE, width), lambda i: (i, 0, 0)),
            pl.BlockSpec(ids_t.shape, lambda i: (0, 0)),
        ],
        out_shape=[
            jax.ShapeDtypeStruct((experts, BODY, width), jnp.bfloat16),
            jax.ShapeDtypeStruct((experts, TILE, width), jnp.bfloat16),
            jax.ShapeDtypeStruct(ids_t.shape, jnp.int32),
        ],
        scratch_shapes=[
            pltpu.VMEM((experts, tok), jnp.float32),
            pltpu.VMEM((group * TAIL, model), jnp.bfloat16),
        ],
        compiler_params=pltpu.CompilerParams(vmem_limit_bytes=14 * MIB),
    )(ids_t, tokens)


def spans(model):
    span = model // PARTS * 2
    return [slice(j * span, (j + 1) * span) for j in range(PARTS // 2)]


def silu_product(gate_act, up_act):
    return (gate_act / (1.0 + jnp.exp(-gate_act)) * up_act).astype(jnp.bfloat16)


def fetches(held, given, sems):
    gate, up, down = held
    copies = []
    for j, part in enumerate(spans(gate.shape[0])):
        copies.append(pltpu.make_async_copy(given[0].at[part, :], gate.at[part, :], sems.at[0, j]))
        copies.append(pltpu.make_async_copy(given[1].at[part, :], up.at[part, :], sems.at[1, j]))
    for j, part in enumerate(spans(gate.shape[0])):
        copies.append(pltpu.make_async_copy(given[2].at[:, part], down.at[:, part], sems.at[2, j]))
    return copies


def held_weights(gate, up, down):
    return [pltpu.VMEM(w.shape, w.dtype) for w in (gate, up, down)] + [pltpu.SemaphoreType.DMA((3, PARTS // 2))]


def main_kernel(x_ref, gate_in, up_in, down_in, y_ref, xs, gate, up, down, sems):
    copies = fetches((gate, up, down), (gate_in, up_in, down_in), sems)

    def first(act, some):
        @pl.when(pl.program_id(0) == 0)
        def _():
            for copy in some:
                act(copy)

    first(lambda copy: copy.start(), copies)
    first(lambda copy: copy.wait(), copies[: PARTS // 2])
    gate_act, up_act = 0.0, 0.0
    for j, part in enumerate(spans(gate.shape[0])):
        main_in(x_ref, xs, j)
        if 2 * j == PARTS // 2:
            first(lambda copy: copy.wait(), copies[PARTS // 2 : PARTS])
        gate_act += dot(xs[:, part], gate[part, :])
        up_act += dot(xs[:, part], up[part, :])
    hidden = silu_product(gate_act, up_act)
    first(lambda copy: copy.wait(), copies[PARTS:])
    for j, part in enumerate(spans(gate.shape[0])):
        main_out(dot(hidden, down[:, part]), y_ref, j)


def main_apply(x, gate, up, down, messages=32):
    count, _, width = x.shape
    model, ff = gate.shape
    block = pl.BlockSpec((messages, BODY, width), lambda i: (i, 0, 0))
    return pl.pallas_call(
        main_kernel,
        grid=(count // messages,),
        in_specs=[block] + [pl.BlockSpec(memory_space=pltpu.HBM)] * 3,
        out_specs=block,
        out_shape=jax.ShapeDtypeStruct((count, ROWS, width), jnp.bfloat16),
        scratch_shapes=[pltpu.VMEM((messages * MAIN, model), jnp.bfloat16)] + held_weights(gate, up, down),
        compiler_params=pltpu.CompilerParams(vmem_limit_bytes=50 * MIB),
        cost_estimate=pl.CostEstimate(
            flops=6 * count * MAIN * model * ff, bytes_accessed=4 * x.size, transcendentals=count * MAIN * ff
        ),
    )(x, gate, up, down)


def tail_kernel(x_ref, gate_in, up_in, down_in, _, y_ref, xs, gate, up, down, sems):
    copies = fetches((gate, up, down), (gate_in, up_in, down_in), sems)
    for copy in copies:
        copy.start()
    tails_in(x_ref, 0, xs, 0)
    gate_act, up_act = 0.0, 0.0
    for j, part in enumerate(spans(gate.shape[0])):
        copies[2 * j].wait()
        copies[2 * j + 1].wait()
        gate_act += dot(xs[:, part], gate[part, :])
        up_act += dot(xs[:, part], up[part, :])
    hidden = silu_product(gate_act, up_act)
    for j, part in enumerate(spans(gate.shape[0])):
        copies[PARTS + j].wait()
        xs[:, part] = dot(hidden, down[:, part]).astype(jnp.bfloat16)
    tails_out(xs, y_ref)


def tail_apply(x, gate, up, down, messages):
    count, _, width = x.shape
    model, ff = gate.shape
    return pl.pallas_call(
        tail_kernel,
        grid=(1,),
        in_specs=[pl.BlockSpec(x.shape, lambda i: (0, 0, 0))] + [pl.BlockSpec(memory_space=pltpu.HBM)] * 4,
        out_specs=pl.BlockSpec(x.shape, lambda i: (0, BODY // TILE, 0)),
        out_shape=jax.ShapeDtypeStruct(messages.shape, jnp.bfloat16),
        scratch_shapes=[pltpu.VMEM((count * TAIL, model), jnp.bfloat16)] + held_weights(gate, up, down),
        input_output_aliases={4: 0},
        compiler_params=pltpu.CompilerParams(vmem_limit_bytes=50 * MIB),
        cost_estimate=pl.CostEstimate(
            flops=6 * count * TAIL * model * ff, bytes_accessed=4 * x.size, transcendentals=count * TAIL * ff
        ),
    )(x, gate, up, down, messages)


def combine_kernel(slot_ref, probs_ref, cot_ref, y_ref, mixed_ref, grads_ref, xs):
    slots, model = xs.shape
    tok = cot_ref.shape[0]
    span = model // PARTS * 2
    here = iota((slots, tok), 0)
    weight = jnp.zeros((slots, tok), jnp.float32)
    for k in range(slot_ref.shape[0]):
        weight += jnp.where(here == slot_ref[k : k + 1, :], probs_ref[k : k + 1, :], 0.0)
    weight = weight.T.astype(jnp.bfloat16)
    tails_in(y_ref, BODY, xs, y_ref.shape[0] * MAIN)
    inner = 0.0
    for j in range(PARTS // 2):
        part = slice(j * span, (j + 1) * span)
        main_in(y_ref, xs, j)
        inner += dot(xs[:, part], cot_ref[:, part], ((1,), (1,)))
        mixed_ref[:, part] = dot(weight, xs[:, part]).astype(jnp.bfloat16)
    for k in range(slot_ref.shape[0]):
        mask = here == slot_ref[k : k + 1, :]
        grads_ref[k : k + 1, :] = jnp.sum(jnp.where(mask, inner, 0.0), axis=0, keepdims=True)


def combine(slot_t, probs_t, cotangent, y):
    model = cotangent.shape[1]
    return pl.pallas_call(
        combine_kernel,
        out_shape=[
            jax.ShapeDtypeStruct(cotangent.shape, jnp.bfloat16),
            jax.ShapeDtypeStruct(probs_t.shape, jnp.float32),
        ],
        scratch_shapes=[pltpu.VMEM((y.shape[0] * CAP, model), jnp.bfloat16)],
        compiler_params=pltpu.CompilerParams(vmem_limit_bytes=40 * MIB),
    )(slot_t, probs_t, cotangent, y)


def exchange(messages):
    return lax.all_to_all(messages, ("node", "local"), split_axis=0, concat_axis=0, tiled=True)


def per_device(tokens, expert_ids, route_probs, cotangent, gate_weight, up_weight, down_weight):
    devices = lax.axis_size("node") * lax.axis_size("local")
    body, tail, slot_t = pack(expert_ids.T, tokens, devices)
    weights = gate_weight[0], up_weight[0], down_weight[0]
    body = exchange(body)
    body, tail = lax.optimization_barrier((body, tail))
    tail = exchange(tail)
    results = tail_apply(tail, *weights, main_apply(body, *weights))
    returned = exchange(results)
    mixed, grads_t = combine(slot_t, route_probs.T, cotangent, returned)
    return mixed, grads_t.T


def solution(mesh):
    placed = (P(("node", "local"), None),) * 4 + (P(("node", "local"), None, None),) * 3
    return jax.shard_map(
        per_device,
        mesh=mesh,
        in_specs=placed,
        out_specs=(P(("node", "local"), None), P(("node", "local"), None)),
        check_vma=False,
    )
```

```python
import functools

import jax
import jax.numpy as jnp
from jax import lax
from jax.experimental import pallas as pl
from jax.experimental.pallas import tpu as pltpu
from jax.sharding import PartitionSpec as P

CAP = 10
PARTS = 8
MAIN = 8
TAIL = CAP - MAIN
TILE = 2 * MAIN
BODY = PARTS * MAIN
ROWS = CAP * PARTS
SUB = 256
MIB = 1 << 20


def iota(shape, dim):
    return lax.broadcasted_iota(jnp.int32, shape, dim)


def dot(a, b, dims=((1,), (0,))):
    return lax.dot_general(a, b, (dims, ((), ())), preferred_element_type=jnp.float32)


def tails_in(x_ref, first, xs, base):
    width = x_ref.shape[2]
    slots = SUB // PARTS
    out, src = iota((SUB, SUB), 0), iota((SUB, SUB), 1)
    order = (src == (out % slots) * PARTS + out // slots).astype(jnp.bfloat16)
    per = SUB // TILE
    for b in range(x_ref.shape[0] // per):
        rows = x_ref[b * per : (b + 1) * per, first : first + TILE, :].reshape(SUB, width)
        rows = dot(order, rows).astype(jnp.bfloat16)
        for q in range(PARTS):
            xs[base + b * slots : base + (b + 1) * slots, q * width : (q + 1) * width] = rows[q * slots : (q + 1) * slots, :]


def tails_out(tails, out_ref):
    width = out_ref.shape[2]
    slots = SUB // PARTS
    out, src = iota((SUB, SUB), 0), iota((SUB, SUB), 1)
    order = (src == (out % PARTS) * slots + out // PARTS).astype(jnp.bfloat16)
    per = SUB // TILE
    for b in range(out_ref.shape[0] // per):
        rows = [tails[b * slots : (b + 1) * slots, q * width : (q + 1) * width] for q in range(PARTS)]
        rows = dot(order, jnp.concatenate(rows, axis=0)).astype(jnp.bfloat16)
        out_ref[b * per : (b + 1) * per, :, :] = rows.reshape(per, TILE, width)


def main_in(x_ref, xs, j, step=32):
    width = x_ref.shape[2]
    for b in range(0, x_ref.shape[0], step):
        both = x_ref[b : b + step, j * TILE : (j + 1) * TILE, :].astype(jnp.float32)
        for half in range(2):
            rows = both[:, half * MAIN : (half + 1) * MAIN, :].reshape(step * MAIN, width)
            q = 2 * j + half
            xs[b * MAIN : (b + step) * MAIN, q * width : (q + 1) * width] = rows.astype(jnp.bfloat16)


def main_out(rows, out_ref, j):
    messages, _, width = out_ref.shape
    halves = [rows[:, h * width : (h + 1) * width].reshape(messages, MAIN, width) for h in range(2)]
    out_ref[:, j * TILE : (j + 1) * TILE, :] = jnp.concatenate(halves, axis=1).astype(jnp.bfloat16)


def pack_kernel(experts, ids_in, tokens_in, body_ref, tail_ref, slot_ref, place, tails, ids_ref, tokens_ref, sems):
    step = pl.program_id(0)
    tok, model = tokens_ref.shape
    group = body_ref.shape[0]
    span = model // PARTS * 2

    @pl.when(step == 0)
    def _():
        ids_copy = pltpu.make_async_copy(ids_in, ids_ref, sems.at[0])
        tokens_copy = pltpu.make_async_copy(tokens_in, tokens_ref, sems.at[1])
        ids_copy.start()
        tokens_copy.start()
        ids_copy.wait()
        ids = ids_ref[...]
        expert = iota((experts, tok), 0)
        named = jnp.zeros((experts, tok), jnp.float32)
        for k in range(ids.shape[0]):
            named += (expert == ids[k : k + 1, :]).astype(jnp.float32)
        before = (iota((tok, tok), 0) < iota((tok, tok), 1)).astype(jnp.bfloat16)
        rank = dot(named.astype(jnp.bfloat16), before)
        place[...] = jnp.where(named > 0.5, rank, -1.0)
        rank = rank.astype(jnp.int32)
        slot_of = jnp.where(rank < MAIN, expert * MAIN + rank, experts * MAIN + expert * TAIL + rank - MAIN)
        for k in range(ids.shape[0]):
            chosen = expert == ids[k : k + 1, :]
            slot_ref[k : k + 1, :] = jnp.sum(jnp.where(chosen, slot_of, 0), axis=0, keepdims=True)
        tokens_copy.wait()

    mine = place[pl.ds(pl.multiple_of(step * group, group), group), :]
    rank = iota((MAIN, tok), 0).astype(jnp.float32)
    main = [(mine[g : g + 1, :] == rank).astype(jnp.float32) for g in range(group)]
    main = jnp.concatenate(main, axis=0).astype(jnp.bfloat16)
    row = iota((MAIN, tok), 0)
    late = []
    for g in range(0, group, MAIN // TAIL):
        match = jnp.zeros((MAIN, tok), jnp.float32)
        for h in range(MAIN // TAIL):
            rank = jnp.where(row // TAIL == h, MAIN + row % TAIL, -2).astype(jnp.float32)
            match += (mine[g + h : g + h + 1, :] == rank).astype(jnp.float32)
        late.append(match)
    late = jnp.concatenate(late, axis=0).astype(jnp.bfloat16)
    for j in range(PARTS // 2):
        part = slice(j * span, (j + 1) * span)
        tails[:, part] = dot(late, tokens_ref[:, part]).astype(jnp.bfloat16)
        main_out(dot(main, tokens_ref[:, part]), body_ref, j)
    tails_out(tails, tail_ref)


def pack(ids_t, tokens, experts):
    tok, model = tokens.shape
    ids_t, tokens = [pltpu.with_memory_space_constraint(a, pltpu.HBM) for a in (ids_t, tokens)]
    group = 32
    width = model // PARTS
    return pl.pallas_call(
        functools.partial(pack_kernel, experts),
        grid=(experts // group,),
        in_specs=[pl.BlockSpec(memory_space=pltpu.HBM)] * 2,
        out_specs=[
            pl.BlockSpec((group, BODY, width), lambda i: (i, 0, 0)),
            pl.BlockSpec((group, TILE, width), lambda i: (i, 0, 0)),
            pl.BlockSpec(ids_t.shape, lambda i: (0, 0)),
        ],
        out_shape=[
            jax.ShapeDtypeStruct((experts, BODY, width), jnp.bfloat16),
            jax.ShapeDtypeStruct((experts, TILE, width), jnp.bfloat16),
            jax.ShapeDtypeStruct(ids_t.shape, jnp.int32),
        ],
        scratch_shapes=[
            pltpu.VMEM((experts, tok), jnp.float32),
            pltpu.VMEM((group * TAIL, model), jnp.bfloat16),
            pltpu.VMEM(ids_t.shape, jnp.int32),
            pltpu.VMEM(tokens.shape, jnp.bfloat16),
            pltpu.SemaphoreType.DMA((2,)),
        ],
        compiler_params=pltpu.CompilerParams(vmem_limit_bytes=14 * MIB),
    )(ids_t, tokens)


def spans(model):
    span = model // PARTS * 2
    return [slice(j * span, (j + 1) * span) for j in range(PARTS // 2)]


def silu_product(gate_act, up_act):
    return (gate_act / (1.0 + jnp.exp(-gate_act)) * up_act).astype(jnp.bfloat16)


def fetches(held, given, sems):
    gate, up, down = held
    copies = []
    for j, part in enumerate(spans(gate.shape[0])):
        copies.append(pltpu.make_async_copy(given[0].at[part, :], gate.at[part, :], sems.at[0, j]))
        copies.append(pltpu.make_async_copy(given[1].at[part, :], up.at[part, :], sems.at[1, j]))
    for j, part in enumerate(spans(gate.shape[0])):
        copies.append(pltpu.make_async_copy(given[2].at[:, part], down.at[:, part], sems.at[2, j]))
    return copies


def held_weights(gate, up, down):
    return [pltpu.VMEM(w.shape, w.dtype) for w in (gate, up, down)] + [pltpu.SemaphoreType.DMA((3, PARTS // 2))]


def main_kernel(x_ref, gate_in, up_in, down_in, y_ref, xs, gate, up, down, sems):
    copies = fetches((gate, up, down), (gate_in, up_in, down_in), sems)

    def first(act, some):
        @pl.when(pl.program_id(0) == 0)
        def _():
            for copy in some:
                act(copy)

    first(lambda copy: copy.start(), copies)
    first(lambda copy: copy.wait(), copies[: PARTS // 2])
    gate_act, up_act = 0.0, 0.0
    for j, part in enumerate(spans(gate.shape[0])):
        main_in(x_ref, xs, j)
        if 2 * j == PARTS // 2:
            first(lambda copy: copy.wait(), copies[PARTS // 2 : PARTS])
        gate_act += dot(xs[:, part], gate[part, :])
        up_act += dot(xs[:, part], up[part, :])
    hidden = silu_product(gate_act, up_act)
    first(lambda copy: copy.wait(), copies[PARTS:])
    for j, part in enumerate(spans(gate.shape[0])):
        main_out(dot(hidden, down[:, part]), y_ref, j)


def main_apply(x, gate, up, down, messages=32):
    count, _, width = x.shape
    model, ff = gate.shape
    block = pl.BlockSpec((messages, BODY, width), lambda i: (i, 0, 0))
    return pl.pallas_call(
        main_kernel,
        grid=(count // messages,),
        in_specs=[block] + [pl.BlockSpec(memory_space=pltpu.HBM)] * 3,
        out_specs=block,
        out_shape=jax.ShapeDtypeStruct((count, ROWS, width), jnp.bfloat16),
        scratch_shapes=[pltpu.VMEM((messages * MAIN, model), jnp.bfloat16)] + held_weights(gate, up, down),
        compiler_params=pltpu.CompilerParams(vmem_limit_bytes=50 * MIB),
        cost_estimate=pl.CostEstimate(
            flops=6 * count * MAIN * model * ff, bytes_accessed=4 * x.size, transcendentals=count * MAIN * ff
        ),
    )(x, gate, up, down)


def tail_kernel(x_ref, gate_in, up_in, down_in, _, y_ref, xs, gate, up, down, sems):
    copies = fetches((gate, up, down), (gate_in, up_in, down_in), sems)
    for copy in copies:
        copy.start()
    tails_in(x_ref, 0, xs, 0)
    gate_act, up_act = 0.0, 0.0
    for j, part in enumerate(spans(gate.shape[0])):
        copies[2 * j].wait()
        copies[2 * j + 1].wait()
        gate_act += dot(xs[:, part], gate[part, :])
        up_act += dot(xs[:, part], up[part, :])
    hidden = silu_product(gate_act, up_act)
    for j, part in enumerate(spans(gate.shape[0])):
        copies[PARTS + j].wait()
        xs[:, part] = dot(hidden, down[:, part]).astype(jnp.bfloat16)
    tails_out(xs, y_ref)


def tail_apply(x, gate, up, down, messages):
    count, _, width = x.shape
    model, ff = gate.shape
    return pl.pallas_call(
        tail_kernel,
        grid=(1,),
        in_specs=[pl.BlockSpec(x.shape, lambda i: (0, 0, 0))] + [pl.BlockSpec(memory_space=pltpu.HBM)] * 4,
        out_specs=pl.BlockSpec(x.shape, lambda i: (0, BODY // TILE, 0)),
        out_shape=jax.ShapeDtypeStruct(messages.shape, jnp.bfloat16),
        scratch_shapes=[pltpu.VMEM((count * TAIL, model), jnp.bfloat16)] + held_weights(gate, up, down),
        input_output_aliases={4: 0},
        compiler_params=pltpu.CompilerParams(vmem_limit_bytes=50 * MIB),
        cost_estimate=pl.CostEstimate(
            flops=6 * count * TAIL * model * ff, bytes_accessed=4 * x.size, transcendentals=count * TAIL * ff
        ),
    )(x, gate, up, down, messages)


def combine_kernel(slot_ref, probs_ref, cot_ref, y_ref, mixed_ref, grads_ref, xs):
    slots, model = xs.shape
    tok = cot_ref.shape[0]
    span = model // PARTS * 2
    here = iota((slots, tok), 0)
    weight = jnp.zeros((slots, tok), jnp.float32)
    for k in range(slot_ref.shape[0]):
        weight += jnp.where(here == slot_ref[k : k + 1, :], probs_ref[k : k + 1, :], 0.0)
    weight = weight.T.astype(jnp.bfloat16)
    tails_in(y_ref, BODY, xs, y_ref.shape[0] * MAIN)
    inner = 0.0
    for j in range(PARTS // 2):
        part = slice(j * span, (j + 1) * span)
        main_in(y_ref, xs, j)
        inner += dot(xs[:, part], cot_ref[:, part], ((1,), (1,)))
        mixed_ref[:, part] = dot(weight, xs[:, part]).astype(jnp.bfloat16)
    for k in range(slot_ref.shape[0]):
        mask = here == slot_ref[k : k + 1, :]
        grads_ref[k : k + 1, :] = jnp.sum(jnp.where(mask, inner, 0.0), axis=0, keepdims=True)


def combine(slot_t, probs_t, cotangent, y):
    model = cotangent.shape[1]
    return pl.pallas_call(
        combine_kernel,
        out_shape=[
            jax.ShapeDtypeStruct(cotangent.shape, jnp.bfloat16),
            jax.ShapeDtypeStruct(probs_t.shape, jnp.float32),
        ],
        scratch_shapes=[pltpu.VMEM((y.shape[0] * CAP, model), jnp.bfloat16)],
        compiler_params=pltpu.CompilerParams(vmem_limit_bytes=40 * MIB),
    )(slot_t, probs_t, cotangent, y)


def exchange(messages):
    return lax.all_to_all(messages, ("node", "local"), split_axis=0, concat_axis=0, tiled=True)


def per_device(tokens, expert_ids, route_probs, cotangent, gate_weight, up_weight, down_weight):
    devices = lax.axis_size("node") * lax.axis_size("local")
    body, tail, slot_t = pack(expert_ids.T, tokens, devices)
    weights = gate_weight[0], up_weight[0], down_weight[0]
    body = exchange(body)
    body, tail = lax.optimization_barrier((body, tail))
    tail = exchange(tail)
    results = tail_apply(tail, *weights, main_apply(body, *weights))
    returned = exchange(results)
    mixed, grads_t = combine(slot_t, route_probs.T, cotangent, returned)
    return mixed, grads_t.T


def solution(mesh):
    placed = (P(("node", "local"), None),) * 4 + (P(("node", "local"), None, None),) * 3
    return jax.shard_map(
        per_device,
        mesh=mesh,
        in_specs=placed,
        out_specs=(P(("node", "local"), None), P(("node", "local"), None)),
        check_vma=False,
    )
```

```python
import functools

import jax
import jax.numpy as jnp
from jax import lax
from jax.experimental import pallas as pl
from jax.experimental.pallas import tpu as pltpu
from jax.sharding import PartitionSpec as P

CAP = 10
PARTS = 8
MAIN = 8
TAIL = CAP - MAIN
TILE = 2 * MAIN
BODY = PARTS * MAIN
ROWS = CAP * PARTS
SUB = 256
MIB = 1 << 20


def iota(shape, dim):
    return lax.broadcasted_iota(jnp.int32, shape, dim)


def dot(a, b, dims=((1,), (0,))):
    return lax.dot_general(a, b, (dims, ((), ())), preferred_element_type=jnp.float32)


def tails_in(x_ref, first, xs, base):
    width = x_ref.shape[2]
    slots = SUB // PARTS
    out, src = iota((SUB, SUB), 0), iota((SUB, SUB), 1)
    order = (src == (out % slots) * PARTS + out // slots).astype(jnp.bfloat16)
    per = SUB // TILE
    for b in range(x_ref.shape[0] // per):
        rows = x_ref[b * per : (b + 1) * per, first : first + TILE, :].reshape(SUB, width)
        rows = dot(order, rows).astype(jnp.bfloat16)
        for q in range(PARTS):
            xs[base + b * slots : base + (b + 1) * slots, q * width : (q + 1) * width] = rows[q * slots : (q + 1) * slots, :]


def tails_out(tails, out_ref):
    width = out_ref.shape[2]
    slots = SUB // PARTS
    out, src = iota((SUB, SUB), 0), iota((SUB, SUB), 1)
    order = (src == (out % PARTS) * slots + out // PARTS).astype(jnp.bfloat16)
    per = SUB // TILE
    for b in range(out_ref.shape[0] // per):
        rows = [tails[b * slots : (b + 1) * slots, q * width : (q + 1) * width] for q in range(PARTS)]
        rows = dot(order, jnp.concatenate(rows, axis=0)).astype(jnp.bfloat16)
        out_ref[b * per : (b + 1) * per, :, :] = rows.reshape(per, TILE, width)


def main_in(x_ref, xs, j, step=32):
    width = x_ref.shape[2]
    for b in range(0, x_ref.shape[0], step):
        both = x_ref[b : b + step, j * TILE : (j + 1) * TILE, :].astype(jnp.float32)
        for half in range(2):
            rows = both[:, half * MAIN : (half + 1) * MAIN, :].reshape(step * MAIN, width)
            q = 2 * j + half
            xs[b * MAIN : (b + step) * MAIN, q * width : (q + 1) * width] = rows.astype(jnp.bfloat16)


def main_out(rows, out_ref, j):
    messages, _, width = out_ref.shape
    halves = [rows[:, h * width : (h + 1) * width].reshape(messages, MAIN, width) for h in range(2)]
    out_ref[:, j * TILE : (j + 1) * TILE, :] = jnp.concatenate(halves, axis=1).astype(jnp.bfloat16)


def pack_kernel(experts, ids_in, tokens_in, body_ref, tail_ref, slot_ref, place, tails, ids_ref, tokens_ref, sems):
    step = pl.program_id(0)
    tok, model = tokens_ref.shape
    group = body_ref.shape[0]
    span = model // PARTS * 2

    @pl.when(step == 0)
    def _():
        ids_copy = pltpu.make_async_copy(ids_in, ids_ref, sems.at[0])
        tokens_copy = pltpu.make_async_copy(tokens_in, tokens_ref, sems.at[1])
        ids_copy.start()
        tokens_copy.start()
        ids_copy.wait()
        ids = ids_ref[...]
        expert = iota((experts, tok), 0)
        named = jnp.zeros((experts, tok), jnp.float32)
        for k in range(ids.shape[0]):
            named += (expert == ids[k : k + 1, :]).astype(jnp.float32)
        before = (iota((tok, tok), 0) < iota((tok, tok), 1)).astype(jnp.bfloat16)
        rank = dot(named.astype(jnp.bfloat16), before)
        place[...] = jnp.where(named > 0.5, rank, -1.0)
        rank = rank.astype(jnp.int32)
        slot_of = jnp.where(rank < MAIN, expert * MAIN + rank, experts * MAIN + expert * TAIL + rank - MAIN)
        for k in range(ids.shape[0]):
            chosen = expert == ids[k : k + 1, :]
            slot_ref[k : k + 1, :] = jnp.sum(jnp.where(chosen, slot_of, 0), axis=0, keepdims=True)
        tokens_copy.wait()

    mine = place[pl.ds(pl.multiple_of(step * group, group), group), :]
    rank = iota((MAIN, tok), 0).astype(jnp.float32)
    main = [(mine[g : g + 1, :] == rank).astype(jnp.float32) for g in range(group)]
    main = jnp.concatenate(main, axis=0).astype(jnp.bfloat16)
    row = iota((MAIN, tok), 0)
    late = []
    for g in range(0, group, MAIN // TAIL):
        match = jnp.zeros((MAIN, tok), jnp.float32)
        for h in range(MAIN // TAIL):
            rank = jnp.where(row // TAIL == h, MAIN + row % TAIL, -2).astype(jnp.float32)
            match += (mine[g + h : g + h + 1, :] == rank).astype(jnp.float32)
        late.append(match)
    late = jnp.concatenate(late, axis=0).astype(jnp.bfloat16)
    for j in range(PARTS // 2):
        part = slice(j * span, (j + 1) * span)
        tails[:, part] = dot(late, tokens_ref[:, part]).astype(jnp.bfloat16)
        main_out(dot(main, tokens_ref[:, part]), body_ref, j)
    tails_out(tails, tail_ref)


def pack(ids_t, tokens, experts):
    tok, model = tokens.shape
    ids_t, tokens = [pltpu.with_memory_space_constraint(a, pltpu.HBM) for a in (ids_t, tokens)]
    group = 32
    width = model // PARTS
    return pl.pallas_call(
        functools.partial(pack_kernel, experts),
        grid=(experts // group,),
        in_specs=[pl.BlockSpec(memory_space=pltpu.HBM)] * 2,
        out_specs=[
            pl.BlockSpec((group, BODY, width), lambda i: (i, 0, 0)),
            pl.BlockSpec((group, TILE, width), lambda i: (i, 0, 0)),
            pl.BlockSpec(ids_t.shape, lambda i: (0, 0)),
        ],
        out_shape=[
            jax.ShapeDtypeStruct((experts, BODY, width), jnp.bfloat16),
            jax.ShapeDtypeStruct((experts, TILE, width), jnp.bfloat16),
            jax.ShapeDtypeStruct(ids_t.shape, jnp.int32),
        ],
        scratch_shapes=[
            pltpu.VMEM((experts, tok), jnp.float32),
            pltpu.VMEM((group * TAIL, model), jnp.bfloat16),
            pltpu.VMEM(ids_t.shape, jnp.int32),
            pltpu.VMEM(tokens.shape, jnp.bfloat16),
            pltpu.SemaphoreType.DMA((2,)),
        ],
        compiler_params=pltpu.CompilerParams(vmem_limit_bytes=14 * MIB),
    )(ids_t, tokens)


def spans(model):
    span = model // PARTS * 2
    return [slice(j * span, (j + 1) * span) for j in range(PARTS // 2)]


def silu_product(gate_act, up_act):
    return (gate_act / (1.0 + jnp.exp(-gate_act)) * up_act).astype(jnp.bfloat16)


def fetches(held, given, sems):
    gate, up, down = held
    copies = []
    for j, part in enumerate(spans(gate.shape[0])):
        copies.append(pltpu.make_async_copy(given[0].at[part, :], gate.at[part, :], sems.at[0, j]))
        copies.append(pltpu.make_async_copy(given[1].at[part, :], up.at[part, :], sems.at[1, j]))
    for j, part in enumerate(spans(gate.shape[0])):
        copies.append(pltpu.make_async_copy(given[2].at[:, part], down.at[:, part], sems.at[2, j]))
    return copies


def held_weights(gate, up, down):
    return [pltpu.VMEM(w.shape, w.dtype) for w in (gate, up, down)] + [pltpu.SemaphoreType.DMA((3, PARTS // 2))]


def main_kernel(x_ref, gate_in, up_in, down_in, slot_ref, probs_ref, y_ref, weight_ref, xs, gate, up, down, sems):
    copies = fetches((gate, up, down), (gate_in, up_in, down_in), sems)

    def first(act, some):
        @pl.when(pl.program_id(0) == 0)
        def _():
            for copy in some:
                act(copy)

    first(lambda copy: copy.start(), copies)

    @pl.when(pl.program_id(0) == 0)
    def _():
        tok, slots = weight_ref.shape
        here = iota((slots, tok), 0)
        weight = jnp.zeros((slots, tok), jnp.float32)
        for k in range(slot_ref.shape[0]):
            weight += jnp.where(here == slot_ref[k : k + 1, :], probs_ref[k : k + 1, :], 0.0)
        weight_ref[...] = weight.T.astype(jnp.bfloat16)

    first(lambda copy: copy.wait(), copies[: PARTS // 2])
    gate_act, up_act = 0.0, 0.0
    for j, part in enumerate(spans(gate.shape[0])):
        main_in(x_ref, xs, j)
        if 2 * j == PARTS // 2:
            first(lambda copy: copy.wait(), copies[PARTS // 2 : PARTS])
        gate_act += dot(xs[:, part], gate[part, :])
        up_act += dot(xs[:, part], up[part, :])
    hidden = silu_product(gate_act, up_act)
    first(lambda copy: copy.wait(), copies[PARTS:])
    for j, part in enumerate(spans(gate.shape[0])):
        main_out(dot(hidden, down[:, part]), y_ref, j)


def main_apply(x, gate, up, down, slot_t, probs_t, messages=32):
    count, _, width = x.shape
    model, ff = gate.shape
    block = pl.BlockSpec((messages, BODY, width), lambda i: (i, 0, 0))
    weight = (slot_t.shape[1], count * CAP)
    whole = lambda shape: pl.BlockSpec(shape, lambda i: (0, 0))
    return pl.pallas_call(
        main_kernel,
        grid=(count // messages,),
        in_specs=[block] + [pl.BlockSpec(memory_space=pltpu.HBM)] * 3 + [whole(slot_t.shape)] * 2,
        out_specs=[block, whole(weight)],
        out_shape=[
            jax.ShapeDtypeStruct((count, ROWS, width), jnp.bfloat16),
            jax.ShapeDtypeStruct(weight, jnp.bfloat16),
        ],
        scratch_shapes=[pltpu.VMEM((messages * MAIN, model), jnp.bfloat16)] + held_weights(gate, up, down),
        compiler_params=pltpu.CompilerParams(vmem_limit_bytes=50 * MIB),
        cost_estimate=pl.CostEstimate(
            flops=6 * count * MAIN * model * ff, bytes_accessed=4 * x.size, transcendentals=count * MAIN * ff
        ),
    )(x, gate, up, down, slot_t, probs_t)


def tail_kernel(x_ref, gate_in, up_in, down_in, _, y_ref, xs, gate, up, down, sems):
    copies = fetches((gate, up, down), (gate_in, up_in, down_in), sems)
    for copy in copies:
        copy.start()
    tails_in(x_ref, 0, xs, 0)
    gate_act, up_act = 0.0, 0.0
    for j, part in enumerate(spans(gate.shape[0])):
        copies[2 * j].wait()
        copies[2 * j + 1].wait()
        gate_act += dot(xs[:, part], gate[part, :])
        up_act += dot(xs[:, part], up[part, :])
    hidden = silu_product(gate_act, up_act)
    for j, part in enumerate(spans(gate.shape[0])):
        copies[PARTS + j].wait()
        xs[:, part] = dot(hidden, down[:, part]).astype(jnp.bfloat16)
    tails_out(xs, y_ref)


def tail_apply(x, gate, up, down, messages):
    count, _, width = x.shape
    model, ff = gate.shape
    return pl.pallas_call(
        tail_kernel,
        grid=(1,),
        in_specs=[pl.BlockSpec(x.shape, lambda i: (0, 0, 0))] + [pl.BlockSpec(memory_space=pltpu.HBM)] * 4,
        out_specs=pl.BlockSpec(x.shape, lambda i: (0, BODY // TILE, 0)),
        out_shape=jax.ShapeDtypeStruct(messages.shape, jnp.bfloat16),
        scratch_shapes=[pltpu.VMEM((count * TAIL, model), jnp.bfloat16)] + held_weights(gate, up, down),
        input_output_aliases={4: 0},
        compiler_params=pltpu.CompilerParams(vmem_limit_bytes=50 * MIB),
        cost_estimate=pl.CostEstimate(
            flops=6 * count * TAIL * model * ff, bytes_accessed=4 * x.size, transcendentals=count * TAIL * ff
        ),
    )(x, gate, up, down, messages)


def combine_kernel(slot_ref, weight_ref, cot_ref, y_ref, mixed_ref, grads_ref, xs):
    slots, model = xs.shape
    tok = cot_ref.shape[0]
    span = model // PARTS * 2
    here = iota((slots, tok), 0)
    weight = weight_ref[...]
    tails_in(y_ref, BODY, xs, y_ref.shape[0] * MAIN)
    inner = 0.0
    for j in range(PARTS // 2):
        part = slice(j * span, (j + 1) * span)
        main_in(y_ref, xs, j)
        inner += dot(xs[:, part], cot_ref[:, part], ((1,), (1,)))
        mixed_ref[:, part] = dot(weight, xs[:, part]).astype(jnp.bfloat16)
    for k in range(slot_ref.shape[0]):
        mask = here == slot_ref[k : k + 1, :]
        grads_ref[k : k + 1, :] = jnp.sum(jnp.where(mask, inner, 0.0), axis=0, keepdims=True)


def combine(slot_t, weight, cotangent, y):
    model = cotangent.shape[1]
    return pl.pallas_call(
        combine_kernel,
        out_shape=[
            jax.ShapeDtypeStruct(cotangent.shape, jnp.bfloat16),
            jax.ShapeDtypeStruct(slot_t.shape, jnp.float32),
        ],
        scratch_shapes=[pltpu.VMEM((y.shape[0] * CAP, model), jnp.bfloat16)],
        compiler_params=pltpu.CompilerParams(vmem_limit_bytes=40 * MIB),
    )(slot_t, weight, cotangent, y)


def exchange(messages):
    return lax.all_to_all(messages, ("node", "local"), split_axis=0, concat_axis=0, tiled=True)


def per_device(tokens, expert_ids, route_probs, cotangent, gate_weight, up_weight, down_weight):
    devices = lax.axis_size("node") * lax.axis_size("local")
    body, tail, slot_t = pack(expert_ids.T, tokens, devices)
    weights = gate_weight[0], up_weight[0], down_weight[0]
    body = exchange(body)
    body, tail = lax.optimization_barrier((body, tail))
    tail = exchange(tail)
    messages, weight = main_apply(body, *weights, slot_t, route_probs.T)
    results = tail_apply(tail, *weights, messages)
    returned = exchange(results)
    mixed, grads_t = combine(slot_t, weight, cotangent, returned)
    return mixed, grads_t.T


def solution(mesh):
    placed = (P(("node", "local"), None),) * 4 + (P(("node", "local"), None, None),) * 3
    return jax.shard_map(
        per_device,
        mesh=mesh,
        in_specs=placed,
        out_specs=(P(("node", "local"), None), P(("node", "local"), None)),
        check_vma=False,
    )
```
